32 devices in a mesh: groups: 2 (over y), mp: 4 (over z), heads: 4 (over x, core).
Axes of the slice: x: 2, y: 2, z: 4, core: 2. Of those that a mesh axis runs over, the one named last changes fastest.
Arguments:
- stream: bfloat16 [16, 8192], P('groups', ('mp', 'heads')), parts along dimension 0, may hold values from -6 to 6
- in_gain: float32 [8192], P('mp'), may hold values from 0.5 to 1.5
- w_inner: bfloat16 [8192, 2, 128, 64], P('mp', None, 'heads'), may hold values from -0.09375 to 0.09375
- w_state: bfloat16 [8192, 2, 4, 256], P('mp'), may hold values from -0.0625 to 0.0625
- w_step: bfloat16 [8192, 128], P('mp', 'heads'), may hold values from -0.0625 to 0.0625
- step_bias: float32 [128], P('heads'), may hold values from -3 to 1
- decay_scale: float32 [128], P('heads'), may hold values from 0.02 to 8
- skip_gain: float32 [128], P('heads'), may hold values from 0.5 to 1.5
- conv_inner: float32 [4, 128, 64], P(None, 'heads', 'mp'), may hold values from -3 to 3
- conv_state_weight: float32 [4, 2, 4, 256], replicated, may hold values from -3 to 3
- history_inner: bfloat16 [16, 3, 128, 64], P('groups', None, 'heads', 'mp'), parts along dimension 0, may hold values from -6 to 6
- history_state: bfloat16 [16, 3, 2, 4, 256], P('groups'), parts along dimension 0, may hold values from -6 to 6
- ssm_state: float32 [16, 128, 64, 256], P('groups', 'heads', 'mp'), parts along dimension 0, may hold values from -4 to 4
- norm_gain: float32 [128, 64], P('heads', 'mp'), may hold values from 0.5 to 1.5
- w_out: bfloat16 [128, 64, 8192], P('heads', None, 'mp'), may hold values from -0.09375 to 0.09375
Outputs:
- residual_out: bfloat16 [8, 16, 8192], P(None, 'groups', ('mp', 'heads')), parts along dimension 1
- state_out: float32 [16, 128, 64, 256], P('groups', 'heads', 'mp'), parts along dimension 0
- inner_hist_out: bfloat16 [16, 3, 128, 64], P('groups', None, 'heads', 'mp'), parts along dimension 0
- state_hist_out: bfloat16 [16, 3, 2, 4, 256], P('groups'), parts along dimension 0
The draws below stay inside these ranges and needn't reach their ends.
There are 2 independent parts, one for each index of `groups`. The reference program is written for one: setup_inputs(seed, part) draws one part's arguments, and reference() takes and returns one part's arrays. A program takes and returns all parts, laid end to end along the dimension named above; an argument that names none is the same for every part. Nothing has to cross between parts.
All inputs are finite; a program needn't handle non-finite values.
Results may differ from the reference program's by a relative error of at most 0.018.
Values may be sent and summed in bfloat16 or wider, within the bound.
A program may use at most 192 MiB of HBM per device.

```python
import math
import jax
import jax.numpy as jnp
from jax import lax

D = 8192
NH = 128
NG = 4
P_SIZE = 64
N = 256
CONV = 4
STEPS = 8
ROWS = 8


def strengthened(values, stream_key, source, target, blocks, factor):
    owner, partner = [(jnp.arange(values.shape[dim]) // (values.shape[dim] // blocks)).reshape([-1 if axis == dim else 1 for axis in range(values.ndim)]) for dim in (source, target)]
    chosen = jax.random.permutation(stream_key, blocks)[partner]
    strong = (owner == chosen) | (owner == (partner + blocks // 2) % blocks)
    return jnp.where(strong, factor * values, values)


def block_scale(stream_key, dims, cuts, least, largest):
    factor_of, own = 1.0, jax.random.fold_in(stream_key, 6)
    for position, shards_of in cuts:
        steps = jnp.exp(jax.random.uniform(jax.random.fold_in(own, position), (shards_of,), jnp.float32, least / len(cuts), largest / len(cuts)))
        factor_of = factor_of * jnp.repeat(steps, dims[position] // shards_of).reshape([-1 if axis == position else 1 for axis in range(len(dims))])
    return factor_of


def centred(rng, extent, deviation, bound, cuts=(), held_as=jnp.bfloat16):
    factor_of = block_scale(rng, extent, cuts, -0.22, 0.18) if cuts else 1.0
    entries = jax.random.normal(rng, extent, jnp.float32) * deviation * factor_of
    return jnp.minimum(jnp.maximum(entries, -bound), bound).astype(held_as)


def gaussian_with(stream_key, extent, scale, bound, split, heavy, held_as=jnp.bfloat16):
    entries = scale * jax.random.normal(stream_key, extent, jnp.float32)
    if split:
        entries = entries * block_scale(stream_key, extent, split, -0.22, 0.18)
    return jnp.clip(strengthened(entries, jax.random.fold_in(stream_key, 3), *heavy), -bound, bound).astype(held_as)


def setup_inputs(seed: int = 0, part: int = 0) -> dict:
    seeds = jax.random.split(jax.random.key(seed), 16)
    part_splits = jax.random.split(jax.random.fold_in(seeds[15], part), 16)
    return {
        "stream": centred(part_splits[0], (ROWS, D), 1.0, 6.0, ((1, 16),)),
        "in_gain": jnp.clip(1.0 + 0.1 * jax.random.normal(seeds[1], (D,), jnp.float32), 0.5, 1.5),
        "w_inner": gaussian_with(seeds[2], (D, 2, NH, P_SIZE), D ** -0.5, 0.09375, ((0, 4), (2, 4)), (0, 3, 4, 2.0)),
        "w_state": centred(seeds[3], (D, 2, NG, N), D ** -0.5, 0.0625, ((0, 4),)),
        "w_step": centred(seeds[4], (D, NH), D ** -0.5, 0.0625, ((0, 4), (1, 4))),
        "step_bias": jnp.clip(-3.0 + 4.0 * jax.random.uniform(seeds[5], (NH,), jnp.float32) ** block_scale(seeds[5], (NH,), ((0, 4),), -0.2, 0.2), -3.0, 1.0),
        "decay_scale": jnp.clip(jnp.exp(math.log(8.0) - 5.9914646 * jax.random.uniform(seeds[6], (NH,), jnp.float32) ** block_scale(seeds[6], (NH,), ((0, 4),), -0.2, 0.2)), 0.02, 8.0),
        "skip_gain": jnp.clip(0.5 + 1.0 * jax.random.uniform(seeds[7], (NH,), jnp.float32) ** block_scale(seeds[7], (NH,), ((0, 4),), -0.2, 0.2), 0.5, 1.5),
        "conv_inner": centred(seeds[8], (CONV, NH, P_SIZE), 0.5, 3.0, ((1, 4), (2, 4)), jnp.float32),
        "conv_state_weight": centred(seeds[9], (CONV, 2, NG, N), 0.5, 3.0, (), jnp.float32),
        "history_inner": centred(part_splits[10], (ROWS, CONV - 1, NH, P_SIZE), 1.0, 6.0, ((2, 4), (3, 4))),
        "history_state": centred(part_splits[11], (ROWS, CONV - 1, 2, NG, N), 1.0, 6.0),
        "ssm_state": centred(part_splits[12], (ROWS, NH, P_SIZE, N), 0.5, 4.0, ((1, 4), (2, 4)), jnp.float32),
        "norm_gain": jnp.clip(1.0 + 0.1 * jax.random.normal(seeds[13], (NH, P_SIZE), jnp.float32), 0.5, 1.5),
        "w_out": gaussian_with(seeds[14], (NH, P_SIZE, D), (NH * P_SIZE) ** -0.5, 0.09375, ((0, 4), (2, 4)), (0, 2, 4, 2.0)),
    }


EPSILON = 1e-05

def causal_conv(history, incoming, kernel):
    window = jnp.concatenate([history, incoming[:, None]], axis=1)
    weighted = lax.optimization_barrier(jnp.sum(window.astype(jnp.float32) * kernel[None], axis=1))
    return (jax.nn.silu(weighted), window[:, 1:])

def reference(stream, in_gain, w_inner, w_state, w_step, step_bias, decay_scale, skip_gain, conv_inner, conv_state_weight, history_inner, history_state, ssm_state, norm_gain, w_out):
    row_count = stream.shape[0]
    per_group = NH // NG
    flat_inner = w_inner.reshape(D, 2 * NH * P_SIZE)
    flat_state = w_state.reshape(D, 2 * NG * N)
    flat_out = w_out.reshape(NH * P_SIZE, D)
    group_of = (jnp.arange(NH) // per_group).astype(jnp.int32)
    current = stream
    hist_inner = history_inner
    hist_state = history_state
    hidden = ssm_state
    written = []
    for step_index in range(STEPS):
        values = current.astype(jnp.float32)
        inv_rms = lax.rsqrt(lax.optimization_barrier(jnp.sum(values * values, axis=1)) / D + EPSILON)[:, None]
        scaled = (values * in_gain[None, :]).astype(jnp.bfloat16)
        proj_inner = jnp.dot(scaled, flat_inner, preferred_element_type=jnp.float32).reshape(row_count, 2, NH, P_SIZE) * inv_rms[:, :, None, None]
        proj_state = jnp.dot(scaled, flat_state, preferred_element_type=jnp.float32) * inv_rms
        proj_step = jnp.dot(scaled, w_step, preferred_element_type=jnp.float32) * inv_rms
        conv_x, hist_inner = causal_conv(hist_inner, proj_inner[:, 0].astype(jnp.bfloat16), conv_inner)
        incoming_bc = proj_state.reshape(row_count, 2, NG, N).astype(jnp.bfloat16)
        conv_bc, hist_state = causal_conv(hist_state, incoming_bc, conv_state_weight)
        head_b = conv_bc[:, 0][:, group_of]
        head_c = conv_bc[:, 1][:, group_of]
        step_dt = jax.nn.softplus(proj_step + step_bias[None, :])
        decay_rate = jnp.exp(-step_dt * decay_scale[None, :])
        hidden = decay_rate[:, :, None, None] * hidden + (step_dt[:, :, None] * conv_x)[:, :, :, None] * head_b[:, :, None, :]
        reading = lax.optimization_barrier(jnp.sum(hidden * head_c[:, :, None, :], axis=3)) + skip_gain[None, :, None] * conv_x
        gated_out = reading * jax.nn.silu(proj_inner[:, 1])
        head_sq = lax.optimization_barrier(jnp.sum(gated_out * gated_out, axis=2))
        group_total = lax.optimization_barrier(jnp.sum(head_sq.reshape(row_count, NG, per_group), axis=2))
        mean_sq = group_total[:, group_of] / (per_group * P_SIZE)
        normed = (gated_out * lax.rsqrt(mean_sq + EPSILON)[:, :, None] * norm_gain[None]).astype(jnp.bfloat16)
        update = jnp.dot(normed.reshape(row_count, NH * P_SIZE), flat_out, preferred_element_type=jnp.float32)
        current = (values + update).astype(jnp.bfloat16)
        written.append(current)
    return (jnp.stack(written), hidden, hist_inner, hist_state)
```

```python
import functools

import jax
import jax.numpy as jnp
from jax import lax
from jax.experimental import pallas as pl
from jax.experimental.pallas import tpu as pltpu
from jax.sharding import PartitionSpec as P

D = 8192
NH = 128
NG = 4
STEPS = 8


EPSILON = 1e-05


def causal_conv(history, incoming, kernel):
    window = jnp.concatenate([history, incoming[:, None]], axis=1)
    weighted = jnp.sum(window.astype(jnp.float32) * kernel[None], axis=1)
    return (jax.nn.silu(weighted), window[:, 1:])


def body(
    stream,
    in_gain,
    w_inner,
    w_state,
    w_step,
    step_bias,
    decay_scale,
    skip_gain,
    conv_inner,
    conv_state_weight,
    history_inner,
    history_state,
    ssm_state,
    norm_gain,
    w_out,
):
    row_count = stream.shape[0]
    local_width = w_inner.shape[0]
    local_heads = w_inner.shape[2]
    head_size = w_inner.shape[3]
    part_size = ssm_state.shape[2]
    group_count = w_state.shape[2]
    state_size = w_state.shape[3]
    flat_inner = w_inner.reshape(local_width, 2 * local_heads * head_size)
    flat_state = w_state.reshape(local_width, 2 * group_count * state_size)
    per_group = NH // NG
    head_ids = lax.axis_index("heads") * local_heads + jnp.arange(local_heads, dtype=jnp.int32)
    member = (head_ids // per_group)[:, None] == jnp.arange(group_count, dtype=jnp.int32)[None, :]
    current = stream
    hist_inner = history_inner
    hist_state = history_state
    hidden = ssm_state
    written = []
    for step_index in range(STEPS):
        values = lax.all_gather(current, "heads", axis=1, tiled=True).astype(jnp.float32)
        scaled = (values * in_gain[None, :]).astype(jnp.bfloat16)
        part_inner = jnp.dot(scaled, flat_inner, preferred_element_type=jnp.float32)
        part_state = jnp.dot(scaled, flat_state, preferred_element_type=jnp.float32)
        part_step = jnp.dot(scaled, w_step, preferred_element_type=jnp.float32)
        part_sq = jnp.sum(values * values, axis=1)
        summed_all, sum_state, sum_step, sum_sq = lax.psum(
            (part_inner, part_state, part_step, part_sq), "mp"
        )
        proj_inner = lax.dynamic_slice_in_dim(
            summed_all.reshape(row_count, 2, local_heads, head_size),
            lax.axis_index("mp") * part_size,
            part_size,
            3,
        )
        inv_rms = lax.rsqrt(sum_sq / D + EPSILON)[:, None]
        proj_inner = proj_inner * inv_rms[:, :, None, None]
        conv_x, hist_inner = causal_conv(
            hist_inner, proj_inner[:, 0].astype(jnp.bfloat16), conv_inner
        )
        incoming_bc = (
            (sum_state * inv_rms)
            .reshape(row_count, 2, group_count, state_size)
            .astype(jnp.bfloat16)
        )
        conv_bc, hist_state = causal_conv(hist_state, incoming_bc, conv_state_weight)
        head_b = jnp.sum(jnp.where(member[None, :, :, None], conv_bc[:, 0][:, None], 0.0), axis=2)
        head_c = jnp.sum(jnp.where(member[None, :, :, None], conv_bc[:, 1][:, None], 0.0), axis=2)
        step_dt = jax.nn.softplus(sum_step * inv_rms + step_bias[None, :])
        decay_rate = jnp.exp(-step_dt * decay_scale[None, :])
        hidden = (
            decay_rate[:, :, None, None] * hidden
            + (step_dt[:, :, None] * conv_x)[:, :, :, None] * head_b[:, :, None, :]
        )
        reading = (
            jnp.sum(hidden * head_c[:, :, None, :], axis=3) + skip_gain[None, :, None] * conv_x
        )
        gated_out = reading * jax.nn.silu(proj_inner[:, 1])
        head_sq = jnp.sum(gated_out * gated_out, axis=2)
        group_part = jnp.sum(jnp.where(member[None], head_sq[:, :, None], 0.0), axis=1)
        group_total = lax.psum(group_part, ("mp", "heads"))
        head_total = jnp.sum(jnp.where(member[None], group_total[:, None, :], 0.0), axis=2)
        mean_sq = head_total / (per_group * head_size)
        normed = (gated_out * lax.rsqrt(mean_sq + EPSILON)[:, :, None] * norm_gain[None]).astype(
            jnp.bfloat16
        )
        partial_out = jnp.einsum(
            "rhp,hpd->rd",
            lax.all_gather(normed, "mp", axis=2, tiled=True),
            w_out,
            preferred_element_type=jnp.float32,
        )
        update = lax.psum_scatter(partial_out, "heads", scatter_dimension=1, tiled=True)
        current = (current.astype(jnp.float32) + update).astype(jnp.bfloat16)
        written.append(current)
    return (jnp.stack(written), hidden, hist_inner, hist_state)


LANES = 128
MESH = pl.DeviceIdType.MESH


def silu(v):
    return v / (1.0 + jnp.exp(-v))


def fused_kernel(
    n_mp,
    n_heads,
    n_local,
    per_head,
    x_ref,
    gain_ref,
    perm_ref,
    spread_ref,
    bias_ref,
    decay_ref,
    skip_ref,
    norm_ref,
    conv_x_ref,
    conv_bc_ref,
    hist_x_in,
    hist_bc_in,
    w_inner_hbm,
    w_aux_hbm,
    w_out_hbm,
    state_hbm,
    out_ref,
    hidden,
    hist_x,
    hist_all,
    w_in,
    w_aux,
    w_o,
    current,
    gathered,
    acc,
    parts,
    part_in,
    norm_out,
    norm_in,
    out_parts,
    out_in,
    hist_bc,
    hist_in,
    reading_s,
    load_sem,
    send_sem,
    recv_sem,
):
    mi = lax.axis_index("mp")
    hi = lax.axis_index("heads")
    rows, feat = x_ref.shape
    chan = norm_ref.shape[1]
    part = w_o.shape[2]
    block = perm_ref.shape[0]
    n_blocks = w_in.shape[2] // block
    n_state = w_aux.shape[2] - LANES
    state_size = n_state // 2

    loads_in = []
    for d in range(n_heads):
        owner = lax.rem(hi - d + n_heads, n_heads)
        span = pl.ds(pl.multiple_of(owner * feat, feat), feat)
        a = pltpu.make_async_copy(w_inner_hbm.at[span], w_in.at[d], load_sem.at[0, d])
        b = pltpu.make_async_copy(w_aux_hbm.at[span], w_aux.at[d], load_sem.at[1, d])
        a.start()
        loads_in.append((a, b))
    for a, b in loads_in:
        b.start()
    loads_rest = [pltpu.make_async_copy(state_hbm, hidden, load_sem.at[2, 0])]
    for d in range(n_mp):
        owner = lax.rem(mi - d + n_mp, n_mp)
        span = pl.ds(pl.multiple_of(owner * part, part), part)
        loads_rest.append(
            pltpu.make_async_copy(w_out_hbm.at[:, span], w_o.at[d], load_sem.at[3, d])
        )
    for c in loads_rest:
        c.start()

    barrier = pltpu.get_barrier_semaphore()
    for d in range(1, n_heads):
        pl.semaphore_signal(
            barrier,
            inc=1,
            device_id={"heads": lax.rem(hi + d, n_heads)},
            device_id_type=MESH,
        )
    for d in range(1, n_mp):
        pl.semaphore_signal(
            barrier, inc=1, device_id={"mp": lax.rem(mi + d, n_mp)}, device_id_type=MESH
        )
    pl.semaphore_wait(barrier, n_heads + n_mp - 2)

    current[...] = x_ref[...]
    hist_x[...] = hist_x_in[...]
    hist_bc[...] = hist_bc_in[...]

    row_chunk = min(feat, 256)
    for d in range(n_heads):
        loads_in[d][0].wait()

        @pl.loop(0, n_blocks)
        def _(b):
            cols = pl.ds(pl.multiple_of(b * block, block), block)
            for r in range(0, feat, row_chunk):
                moved = jnp.dot(
                    w_in[d, r : r + row_chunk, cols],
                    perm_ref[...],
                    preferred_element_type=jnp.float32,
                )
                w_in[d, r : r + row_chunk, cols] = moved.astype(jnp.bfloat16)

    for a, b in loads_in:
        b.wait()
    for c in loads_rest:
        c.wait()

    def exchange(phase, axis, me, n, source, dest):
        copies = []
        for d in range(1, n):
            target = lax.rem(me + d, n)
            c = pltpu.make_async_remote_copy(
                src_ref=source(target),
                dst_ref=dest.at[d],
                send_sem=send_sem.at[phase, d],
                recv_sem=recv_sem.at[phase, d],
                device_id={axis: target},
                device_id_type=MESH,
            )
            c.start()
            copies.append(c)
        return copies

    chunk = block

    def step(s, carry):
        cur = current[...]
        sent = exchange(0, "heads", hi, n_heads, lambda t: current, gathered)
        first = (cur * gain_ref[hi]).astype(jnp.bfloat16)
        sq = jnp.sum(cur * cur, axis=1, keepdims=True)
        for b in range(n_blocks):
            lo = b * chunk
            acc[:, lo : lo + chunk] = jnp.dot(
                first, w_in[0, :, lo : lo + chunk], preferred_element_type=jnp.float32
            )
        aux = jnp.dot(first, w_aux[0], preferred_element_type=jnp.float32)
        later = []
        for d in range(1, n_heads):
            sent[d - 1].wait()
            v = gathered[d]
            owner = lax.rem(hi - d + n_heads, n_heads)
            later.append((v * gain_ref[owner]).astype(jnp.bfloat16))
            sq = sq + jnp.sum(v * v, axis=1, keepdims=True)
        for b in range(n_blocks):
            lo = b * chunk
            total = acc[:, lo : lo + chunk]
            for d in range(1, n_heads):
                total = total + jnp.dot(
                    later[d - 1],
                    w_in[d, :, lo : lo + chunk],
                    preferred_element_type=jnp.float32,
                )
            for m in range(n_mp):
                parts[m, :, b * LANES : (b + 1) * LANES] = total[:, m * LANES : (m + 1) * LANES]
        for d in range(1, n_heads):
            aux = aux + jnp.dot(later[d - 1], w_aux[d], preferred_element_type=jnp.float32)
        lane = lax.broadcasted_iota(jnp.int32, (rows, LANES), 1)
        tail = jnp.where(lane == n_local, sq, aux[:, n_state:])
        for m in range(n_mp):
            parts[m, :, 2 * chan : 2 * chan + n_state] = aux[:, :n_state]
            parts[m, :, 2 * chan + n_state :] = tail

        sent = exchange(1, "mp", mi, n_mp, lambda t: parts.at[t], part_in)
        total = parts[mi]
        for d in range(1, n_mp):
            sent[d - 1].wait()
            total = total + part_in[d]
        tail = total[:, 2 * chan + n_state :]
        inv = lax.rsqrt(tail[:, n_local : n_local + 1] / D + EPSILON)
        new_x = (total[:, :chan] * inv).astype(jnp.bfloat16).astype(jnp.float32)
        gate = total[:, chan : 2 * chan] * inv
        new_bc = (
            (total[:, 2 * chan : 2 * chan + n_state] * inv)
            .astype(jnp.bfloat16)
            .astype(jnp.float32)
        )

        def conv(hist, new, kernel):
            old = [hist[0], hist[1], hist[2]]
            hist[0] = old[1]
            hist[1] = old[2]
            hist[2] = new
            v = old[0] * kernel[0] + old[1] * kernel[1] + old[2] * kernel[2] + new * kernel[3]
            return silu(v)

        conv_x = conv(hist_x, new_x, conv_x_ref)
        conv_bc = conv(hist_bc, new_bc, conv_bc_ref)
        spread = jnp.dot(
            tail,
            spread_ref[...],
            preferred_element_type=jnp.float32,
            precision=lax.Precision.HIGHEST,
        )
        raw = spread * inv + bias_ref[...]
        dt = jnp.maximum(raw, 0.0) + jnp.log1p(jnp.exp(-jnp.abs(raw)))
        decay = jnp.exp(-dt * decay_ref[...])
        driven = dt * conv_x
        b_cols = jnp.transpose(conv_bc[:, :state_size])
        c_cols = jnp.transpose(conv_bc[:, state_size:])
        part_n = min(state_size, 64)
        for r in range(rows):
            sums = [jnp.zeros((part_n, LANES), jnp.float32) for _ in range(chan // LANES)]
            for n0 in range(0, state_size, part_n):
                b_wide = jnp.broadcast_to(b_cols[n0 : n0 + part_n, r : r + 1], (part_n, LANES))
                c_wide = jnp.broadcast_to(c_cols[n0 : n0 + part_n, r : r + 1], (part_n, LANES))
                for c in range(chan // LANES):
                    cols = slice(c * LANES, (c + 1) * LANES)
                    h = (
                        decay[r : r + 1, cols] * hidden[r, n0 : n0 + part_n, cols]
                        + driven[r : r + 1, cols] * b_wide
                    )
                    hidden[r, n0 : n0 + part_n, cols] = h
                    sums[c] = sums[c] + h * c_wide
            for c in range(chan // LANES):
                reading_s[r : r + 1, c * LANES : (c + 1) * LANES] = jnp.sum(
                    sums[c], axis=0, keepdims=True
                )
        reading = reading_s[...] + skip_ref[...] * conv_x
        gated = reading * silu(gate)
        group_sq = jnp.sum(gated * gated, axis=1, keepdims=True)
        mine = (gated * norm_ref[...]).astype(jnp.bfloat16)
        norm_out[:, :chan] = mine.astype(jnp.float32)
        norm_out[:, chan:] = jnp.broadcast_to(group_sq, (rows, LANES))

        sent = exchange(2, "mp", mi, n_mp, lambda t: norm_out, norm_in)

        def out_weight(d, b):
            w = w_o[d, :, :, b * feat : (b + 1) * feat]
            return w.reshape(w.shape[0] * w.shape[1], feat)

        for b in range(n_heads):
            out_parts[b] = jnp.dot(mine, out_weight(0, b), preferred_element_type=jnp.float32)
        later = []
        for d in range(1, n_mp):
            sent[d - 1].wait()
            later.append(norm_in[d, :, :chan].astype(jnp.bfloat16))
            group_sq = group_sq + norm_in[d, :, chan : chan + 1]
        scale = lax.rsqrt(group_sq / (n_local * per_head) + EPSILON)
        for b in range(n_heads):
            total = out_parts[b]
            for d in range(1, n_mp):
                total = total + jnp.dot(
                    later[d - 1], out_weight(d, b), preferred_element_type=jnp.float32
                )
            out_parts[b] = total * scale

        sent = exchange(3, "heads", hi, n_heads, lambda t: out_parts.at[t], out_in)
        update = out_parts[hi]
        for d in range(1, n_heads):
            sent[d - 1].wait()
            update = update + out_in[d]
        new = (cur + update).astype(jnp.bfloat16).astype(jnp.float32)
        current[...] = new
        out_ref[s] = new
        return carry

    lax.fori_loop(0, STEPS, step, 0)

    sent = exchange(4, "heads", hi, n_heads, lambda t: hist_bc, hist_in)
    hist_all[hi] = hist_bc[...]
    for d in range(1, n_heads):
        sent[d - 1].wait()
        hist_all[lax.rem(hi - d + n_heads, n_heads)] = hist_in[d]


def fused_body(
    n_mp,
    n_heads,
    stream,
    in_gain,
    w_inner,
    w_state,
    w_step,
    step_bias,
    decay_scale,
    skip_gain,
    conv_inner,
    conv_state_weight,
    history_inner,
    history_state,
    ssm_state,
    norm_gain,
    w_out,
):
    f32, bf16 = jnp.float32, jnp.bfloat16
    rows, feat = stream.shape
    width, _, n_local, per_head = w_inner.shape
    part = ssm_state.shape[2]
    state_size = w_state.shape[3]
    n_groups = w_state.shape[2]
    chan = n_local * part
    n_state = 2 * state_size
    hi = lax.axis_index("heads")
    in_block = LANES // part
    block = in_block * per_head
    i_in = jnp.arange(block)
    head, slot, lane = i_in // per_head, (i_in % per_head) // part, i_in % part
    place = slot * LANES + head * part + lane
    perm = (place[:, None] == jnp.arange(block)[None, :]).astype(bf16)
    spread = (jnp.arange(LANES)[:, None] == (jnp.arange(chan) // part)[None, :]).astype(f32)
    own_state = lax.dynamic_slice_in_dim(w_state, hi, 1, 2).reshape(width, n_state)
    aux = jnp.concatenate([own_state, jnp.pad(w_step, ((0, 0), (0, LANES - n_local)))], axis=1)
    wide = lambda v: jnp.repeat(v, part)[None]
    own_conv = lax.dynamic_slice_in_dim(conv_state_weight, hi, 1, 2).reshape(4, 1, n_state)
    own_hist = lax.dynamic_slice_in_dim(history_state, hi, 1, 3).reshape(rows, 3, n_state)
    vmem = pl.BlockSpec(memory_space=pltpu.VMEM)
    hbm = pl.BlockSpec(memory_space=pl.ANY)
    shape = jax.ShapeDtypeStruct
    out, hidden, hist_x, hist_bc = pl.pallas_call(
        functools.partial(fused_kernel, n_mp, n_heads, n_local, per_head),
        out_shape=(
            shape((STEPS, rows, feat), f32),
            shape((rows, state_size, chan), f32),
            shape((3, rows, chan), f32),
            shape((n_heads, 3, rows, n_state), f32),
        ),
        in_specs=[vmem] * 12 + [hbm] * 4,
        out_specs=(vmem,) * 4,
        scratch_shapes=[
            pltpu.VMEM((n_heads, feat, 2 * n_local * per_head), bf16),
            pltpu.VMEM((n_heads, feat, n_state + LANES), bf16),
            pltpu.VMEM((n_mp, n_local, part, w_out.shape[2]), bf16),
            pltpu.VMEM((rows, feat), f32),
            pltpu.VMEM((n_heads, rows, feat), f32),
            pltpu.VMEM((rows, 2 * n_local * per_head), f32),
            pltpu.VMEM((n_mp, rows, 2 * chan + n_state + LANES), f32),
            pltpu.VMEM((n_mp, rows, 2 * chan + n_state + LANES), f32),
            pltpu.VMEM((rows, chan + LANES), f32),
            pltpu.VMEM((n_mp, rows, chan + LANES), f32),
            pltpu.VMEM((n_heads, rows, feat), f32),
            pltpu.VMEM((n_heads, rows, feat), f32),
            pltpu.VMEM((3, rows, n_state), f32),
            pltpu.VMEM((n_heads, 3, rows, n_state), f32),
            pltpu.VMEM((rows, chan), f32),
            pltpu.SemaphoreType.DMA((4, max(n_mp, n_heads))),
            pltpu.SemaphoreType.DMA((5, max(n_mp, n_heads))),
            pltpu.SemaphoreType.DMA((5, max(n_mp, n_heads))),
        ],
        compiler_params=pltpu.CompilerParams(
            collective_id=0, has_side_effects=True, vmem_limit_bytes=56 * 1024 * 1024
        ),
    )(
        stream.astype(f32),
        in_gain.reshape(n_heads, 1, feat),
        perm,
        spread,
        wide(step_bias),
        wide(decay_scale),
        wide(skip_gain),
        norm_gain.reshape(1, chan),
        conv_inner.reshape(4, 1, chan),
        own_conv,
        jnp.swapaxes(history_inner.reshape(rows, 3, chan), 0, 1).astype(f32),
        jnp.swapaxes(own_hist, 0, 1).astype(f32),
        w_inner.reshape(width, 2 * n_local * per_head),
        aux,
        w_out,
        jnp.swapaxes(ssm_state.reshape(rows, chan, state_size), 1, 2),
    )
    hist_bc = hist_bc.reshape(n_groups, 3, rows, 2, state_size).transpose(2, 1, 3, 0, 4)
    return (
        out.astype(bf16),
        jnp.swapaxes(hidden, 1, 2).reshape(ssm_state.shape),
        jnp.swapaxes(hist_x, 0, 1).reshape(history_inner.shape).astype(bf16),
        hist_bc.astype(bf16),
    )


def choose_body(n_mp, n_heads):
    def run(*args):
        stream, w_inner, w_state, ssm_state = args[0], args[2], args[3], args[12]
        n_local, per_head = w_inner.shape[2], w_inner.shape[3]
        part = ssm_state.shape[2]
        aligned = (
            n_local == NH // NG
            and n_heads == w_state.shape[2]
            and n_local < LANES
            and LANES % part == 0
            and per_head == part * n_mp
            and (n_local * part) % LANES == 0
            and stream.shape[1] % LANES == 0
            and w_state.shape[3] % LANES == 0
        )
        if aligned:
            return fused_body(n_mp, n_heads, *args)
        return body(*args)

    return run


def solution(mesh):
    return jax.shard_map(
        choose_body(mesh.shape["mp"], mesh.shape["heads"]),
        mesh=mesh,
        in_specs=(
            P("groups", ("mp", "heads")),
            P("mp"),
            P("mp", None, "heads", None),
            P("mp", None, None, None),
            P("mp", "heads"),
            P("heads"),
            P("heads"),
            P("heads"),
            P(None, "heads", "mp"),
            P(),
            P("groups", None, "heads", "mp"),
            P("groups", None, None, None, None),
            P("groups", "heads", "mp", None),
            P("heads", "mp"),
            P("heads", None, "mp"),
        ),
        out_specs=(
            P(None, "groups", ("mp", "heads")),
            P("groups", "heads", "mp", None),
            P("groups", None, "heads", "mp"),
            P("groups", None, None, None, None),
        ),
        check_vma=False,
    )
```

```python
import functools

import jax
import jax.numpy as jnp
import numpy as np
from jax import lax
from jax.experimental import pallas as pl
from jax.experimental.pallas import tpu as pltpu
from jax.sharding import PartitionSpec as P

D = 8192
NH = 128
NG = 4
STEPS = 8


EPSILON = 1e-05


def causal_conv(history, incoming, kernel):
    window = jnp.concatenate([history, incoming[:, None]], axis=1)
    weighted = jnp.sum(window.astype(jnp.float32) * kernel[None], axis=1)
    return (jax.nn.silu(weighted), window[:, 1:])


def body(
    stream,
    in_gain,
    w_inner,
    w_state,
    w_step,
    step_bias,
    decay_scale,
    skip_gain,
    conv_inner,
    conv_state_weight,
    history_inner,
    history_state,
    ssm_state,
    norm_gain,
    w_out,
):
    row_count = stream.shape[0]
    local_width = w_inner.shape[0]
    local_heads = w_inner.shape[2]
    head_size = w_inner.shape[3]
    part_size = ssm_state.shape[2]
    group_count = w_state.shape[2]
    state_size = w_state.shape[3]
    flat_inner = w_inner.reshape(local_width, 2 * local_heads * head_size)
    flat_state = w_state.reshape(local_width, 2 * group_count * state_size)
    per_group = NH // NG
    head_ids = lax.axis_index("heads") * local_heads + jnp.arange(local_heads, dtype=jnp.int32)
    member = (head_ids // per_group)[:, None] == jnp.arange(group_count, dtype=jnp.int32)[None, :]
    current = stream
    hist_inner = history_inner
    hist_state = history_state
    hidden = ssm_state
    written = []
    for step_index in range(STEPS):
        values = lax.all_gather(current, "heads", axis=1, tiled=True).astype(jnp.float32)
        scaled = (values * in_gain[None, :]).astype(jnp.bfloat16)
        part_inner = jnp.dot(scaled, flat_inner, preferred_element_type=jnp.float32)
        part_state = jnp.dot(scaled, flat_state, preferred_element_type=jnp.float32)
        part_step = jnp.dot(scaled, w_step, preferred_element_type=jnp.float32)
        part_sq = jnp.sum(values * values, axis=1)
        summed_all, sum_state, sum_step, sum_sq = lax.psum(
            (part_inner, part_state, part_step, part_sq), "mp"
        )
        proj_inner = lax.dynamic_slice_in_dim(
            summed_all.reshape(row_count, 2, local_heads, head_size),
            lax.axis_index("mp") * part_size,
            part_size,
            3,
        )
        inv_rms = lax.rsqrt(sum_sq / D + EPSILON)[:, None]
        proj_inner = proj_inner * inv_rms[:, :, None, None]
        conv_x, hist_inner = causal_conv(
            hist_inner, proj_inner[:, 0].astype(jnp.bfloat16), conv_inner
        )
        incoming_bc = (
            (sum_state * inv_rms)
            .reshape(row_count, 2, group_count, state_size)
            .astype(jnp.bfloat16)
        )
        conv_bc, hist_state = causal_conv(hist_state, incoming_bc, conv_state_weight)
        head_b = jnp.sum(jnp.where(member[None, :, :, None], conv_bc[:, 0][:, None], 0.0), axis=2)
        head_c = jnp.sum(jnp.where(member[None, :, :, None], conv_bc[:, 1][:, None], 0.0), axis=2)
        step_dt = jax.nn.softplus(sum_step * inv_rms + step_bias[None, :])
        decay_rate = jnp.exp(-step_dt * decay_scale[None, :])
        hidden = (
            decay_rate[:, :, None, None] * hidden
            + (step_dt[:, :, None] * conv_x)[:, :, :, None] * head_b[:, :, None, :]
        )
        reading = (
            jnp.sum(hidden * head_c[:, :, None, :], axis=3) + skip_gain[None, :, None] * conv_x
        )
        gated_out = reading * jax.nn.silu(proj_inner[:, 1])
        head_sq = jnp.sum(gated_out * gated_out, axis=2)
        group_part = jnp.sum(jnp.where(member[None], head_sq[:, :, None], 0.0), axis=1)
        group_total = lax.psum(group_part, ("mp", "heads"))
        head_total = jnp.sum(jnp.where(member[None], group_total[:, None, :], 0.0), axis=2)
        mean_sq = head_total / (per_group * head_size)
        normed = (gated_out * lax.rsqrt(mean_sq + EPSILON)[:, :, None] * norm_gain[None]).astype(
            jnp.bfloat16
        )
        partial_out = jnp.einsum(
            "rhp,hpd->rd",
            lax.all_gather(normed, "mp", axis=2, tiled=True),
            w_out,
            preferred_element_type=jnp.float32,
        )
        update = lax.psum_scatter(partial_out, "heads", scatter_dimension=1, tiled=True)
        current = (current.astype(jnp.float32) + update).astype(jnp.bfloat16)
        written.append(current)
    return (jnp.stack(written), hidden, hist_inner, hist_state)


LANES = 128
MESH = pl.DeviceIdType.MESH


def silu(v):
    return v / (1.0 + jnp.exp(-v))


def fused_kernel(
    n_mp,
    n_heads,
    n_local,
    per_head,
    x_ref,
    gain_ref,
    spread_ref,
    pack_ref,
    pack_bc_ref,
    w_inner_hbm,
    w_state_hbm,
    w_step_hbm,
    w_out_hbm,
    state_hbm,
    out_ref,
    hidden,
    hist_x,
    hist_all,
    w_in,
    w_st,
    w_dt,
    w_o,
    current,
    gathered,
    parts,
    part_in,
    norm_out,
    norm_in,
    out_parts,
    out_in,
    hist_bc,
    hist_in,
    reading_s,
    load_sem,
    send_sem,
    recv_sem,
):
    mi = lax.axis_index("mp")
    hi = lax.axis_index("heads")
    rows, feat = x_ref.shape
    part = w_o.shape[2]
    chan = n_local * part
    n_state = w_st.shape[1]
    state_size = n_state // 2

    w_dt[...] = jnp.zeros_like(w_dt)
    loads_in = []
    for d in range(n_heads):
        owner = lax.rem(hi - d + n_heads, n_heads)
        span = pl.ds(pl.multiple_of(owner * feat, feat), feat)
        copies = [
            pltpu.make_async_copy(
                w_inner_hbm.at[:, :, m * part : (m + 1) * part, span],
                w_in.at[d, m],
                load_sem.at[4 + m, d],
            )
            for m in range(n_mp)
        ]
        copies.append(pltpu.make_async_copy(w_state_hbm.at[:, span], w_st.at[d], load_sem.at[0, d]))
        copies.append(
            pltpu.make_async_copy(
                w_step_hbm.at[:, span], w_dt.at[d, 0:n_local], load_sem.at[1, d]
            )
        )
        for c in copies:
            c.start()
        loads_in.append(copies)
    load_state = pltpu.make_async_copy(state_hbm, hidden, load_sem.at[2, 0])
    load_state.start()
    loads_out = []
    for d in range(n_mp):
        owner = lax.rem(mi - d + n_mp, n_mp)
        span = pl.ds(pl.multiple_of(owner * part, part), part)
        c = pltpu.make_async_copy(w_out_hbm.at[:, span], w_o.at[d], load_sem.at[3, d])
        c.start()
        loads_out.append(c)

    barrier = pltpu.get_barrier_semaphore()
    for d in range(1, n_heads):
        pl.semaphore_signal(
            barrier,
            inc=1,
            device_id={"heads": lax.rem(hi + d, n_heads)},
            device_id_type=MESH,
        )
    for d in range(1, n_mp):
        pl.semaphore_signal(
            barrier, inc=1, device_id={"mp": lax.rem(mi + d, n_mp)}, device_id_type=MESH
        )
    pl.semaphore_wait(barrier, n_heads + n_mp - 2)

    current[...] = x_ref[...]
    for k in range(3):
        hist_x[k] = pack_ref[8 + k * rows : 8 + (k + 1) * rows]
        hist_bc[k] = pack_bc_ref[8 + k * rows : 8 + (k + 1) * rows]

    def exchange(phase, axis, me, n, source, dest):
        copies = []
        for d in range(1, n):
            target = lax.rem(me + d, n)
            c = pltpu.make_async_remote_copy(
                src_ref=source(target),
                dst_ref=dest.at[d],
                send_sem=send_sem.at[phase, d],
                recv_sem=recv_sem.at[phase, d],
                device_id={axis: target},
                device_id_type=MESH,
            )
            c.start()
            copies.append(c)
        return copies

    def in_dot(x, w):
        return lax.dot_general(
            x, w, (((1,), (1,)), ((), ())), preferred_element_type=jnp.float32
        )

    def in_weight(d, m):
        return w_in[d, m].reshape(2 * chan, feat)

    def step(s, carry):
        cur = current[...]
        sent = exchange(0, "heads", hi, n_heads, lambda t: current, gathered)
        first = (cur * gain_ref[hi]).astype(jnp.bfloat16)
        sq = jnp.sum(cur * cur, axis=1, keepdims=True)

        @pl.when(s == 0)
        def _():
            for c in loads_in[0]:
                c.wait()

        for m in range(n_mp):
            parts[m, :, : 2 * chan] = in_dot(first, in_weight(0, m))
        aux = in_dot(first, w_st[0])
        tail = in_dot(first, w_dt[0])
        later = []
        for d in range(1, n_heads):
            sent[d - 1].wait()
            v = gathered[d]
            owner = lax.rem(hi - d + n_heads, n_heads)
            later.append((v * gain_ref[owner]).astype(jnp.bfloat16))
            sq = sq + jnp.sum(v * v, axis=1, keepdims=True)

        @pl.when(s == 0)
        def _():
            for copies in loads_in[1:]:
                for c in copies:
                    c.wait()

        for m in range(n_mp):
            total = parts[m, :, : 2 * chan]
            for d in range(1, n_heads):
                total = total + in_dot(later[d - 1], in_weight(d, m))
            parts[m, :, : 2 * chan] = total
        for d in range(1, n_heads):
            aux = aux + in_dot(later[d - 1], w_st[d])
            tail = tail + in_dot(later[d - 1], w_dt[d])
        lane = lax.broadcasted_iota(jnp.int32, (rows, LANES), 1)
        tail = jnp.where(lane == n_local, sq, tail)
        for m in range(n_mp):
            parts[m, :, 2 * chan : 2 * chan + n_state] = aux
            parts[m, :, 2 * chan + n_state :] = tail

        sent = exchange(1, "mp", mi, n_mp, lambda t: parts.at[t], part_in)
        total = parts[mi]
        for d in range(1, n_mp):
            sent[d - 1].wait()
            total = total + part_in[d]
        tail = total[:, 2 * chan + n_state :]
        inv = lax.rsqrt(tail[:, n_local : n_local + 1] / D + EPSILON)
        new_x = (total[:, :chan] * inv).astype(jnp.bfloat16).astype(jnp.float32)
        gate = total[:, chan : 2 * chan] * inv
        new_bc = (
            (total[:, 2 * chan : 2 * chan + n_state] * inv)
            .astype(jnp.bfloat16)
            .astype(jnp.float32)
        )

        def conv(hist, new, kernel):
            old = [hist[0], hist[1], hist[2]]
            hist[0] = old[1]
            hist[1] = old[2]
            hist[2] = new
            v = old[0] * kernel[0:1] + old[1] * kernel[1:2] + old[2] * kernel[2:3] + new * kernel[3:4]
            return silu(v)

        conv_x = conv(hist_x, new_x, pack_ref)
        conv_bc = conv(hist_bc, new_bc, pack_bc_ref)
        spread = jnp.dot(
            tail,
            spread_ref[...],
            preferred_element_type=jnp.float32,
            precision=lax.Precision.HIGHEST,
        )
        raw = spread * inv + pack_ref[5:6]
        dt = jnp.maximum(raw, 0.0) + jnp.log1p(jnp.exp(-jnp.abs(raw)))
        decay = jnp.exp(-dt * pack_ref[6:7])
        driven = dt * conv_x
        b_cols = jnp.transpose(conv_bc[:, :state_size])
        c_cols = jnp.transpose(conv_bc[:, state_size:])
        part_n = min(state_size, 64)

        @pl.when(s == 0)
        def _():
            load_state.wait()

        for r in range(rows):
            sums = [jnp.zeros((part_n, LANES), jnp.float32) for _ in range(chan // LANES)]
            for n0 in range(0, state_size, part_n):
                b_wide = jnp.broadcast_to(b_cols[n0 : n0 + part_n, r : r + 1], (part_n, LANES))
                c_wide = jnp.broadcast_to(c_cols[n0 : n0 + part_n, r : r + 1], (part_n, LANES))
                for c in range(chan // LANES):
                    cols = slice(c * LANES, (c + 1) * LANES)
                    h = (
                        decay[r : r + 1, cols] * hidden[r, n0 : n0 + part_n, cols]
                        + driven[r : r + 1, cols] * b_wide
                    )
                    hidden[r, n0 : n0 + part_n, cols] = h
                    sums[c] = sums[c] + h * c_wide
            for c in range(chan // LANES):
                reading_s[r : r + 1, c * LANES : (c + 1) * LANES] = jnp.sum(
                    sums[c], axis=0, keepdims=True
                )
        reading = reading_s[...] + pack_ref[7:8] * conv_x
        gated = reading * silu(gate)
        group_sq = jnp.sum(gated * gated, axis=1, keepdims=True)
        mine = (gated * pack_ref[4:5]).astype(jnp.bfloat16)
        norm_out[:, :chan] = mine.astype(jnp.float32)
        norm_out[:, chan:] = jnp.broadcast_to(group_sq, (rows, LANES))

        sent = exchange(2, "mp", mi, n_mp, lambda t: norm_out, norm_in)

        def out_weight(d, b):
            w = w_o[d, :, :, b * feat : (b + 1) * feat]
            return w.reshape(w.shape[0] * w.shape[1], feat)

        @pl.when(s == 0)
        def _():
            for c in loads_out:
                c.wait()

        for b in range(n_heads):
            out_parts[b] = jnp.dot(mine, out_weight(0, b), preferred_element_type=jnp.float32)
        later = []
        for d in range(1, n_mp):
            sent[d - 1].wait()
            later.append(norm_in[d, :, :chan].astype(jnp.bfloat16))
            group_sq = group_sq + norm_in[d, :, chan : chan + 1]
        scale = lax.rsqrt(group_sq / (n_local * per_head) + EPSILON)
        for b in range(n_heads):
            total = out_parts[b]
            for d in range(1, n_mp):
                total = total + jnp.dot(
                    later[d - 1], out_weight(d, b), preferred_element_type=jnp.float32
                )
            out_parts[b] = total * scale

        sent = exchange(3, "heads", hi, n_heads, lambda t: out_parts.at[t], out_in)
        update = out_parts[hi]
        for d in range(1, n_heads):
            sent[d - 1].wait()
            update = update + out_in[d]
        new = (cur + update).astype(jnp.bfloat16).astype(jnp.float32)
        current[...] = new
        out_ref[s] = new
        return carry

    lax.fori_loop(0, STEPS, step, 0)

    sent = exchange(4, "heads", hi, n_heads, lambda t: hist_bc, hist_in)
    hist_all[hi] = hist_bc[...]
    for d in range(1, n_heads):
        sent[d - 1].wait()
        hist_all[lax.rem(hi - d + n_heads, n_heads)] = hist_in[d]


def fused_body(
    n_mp,
    n_heads,
    stream,
    in_gain,
    w_inner,
    w_state,
    w_step,
    step_bias,
    decay_scale,
    skip_gain,
    conv_inner,
    conv_state_weight,
    history_inner,
    history_state,
    ssm_state,
    norm_gain,
    w_out,
):
    f32, bf16 = jnp.float32, jnp.bfloat16
    rows, feat = stream.shape
    width, _, n_local, per_head = w_inner.shape
    part = ssm_state.shape[2]
    state_size = w_state.shape[3]
    n_groups = w_state.shape[2]
    chan = n_local * part
    n_state = 2 * state_size
    hi = lax.axis_index("heads")
    spread = (np.arange(LANES)[:, None] == (np.arange(chan) // part)[None, :]).astype(np.float32)
    own_state = lax.dynamic_slice_in_dim(w_state, hi, 1, 2).reshape(width, n_state)
    heads_wide = jnp.stack([step_bias, decay_scale, skip_gain])
    pack = jnp.concatenate(
        [
            conv_inner,
            norm_gain[None],
            jnp.broadcast_to(heads_wide[:, :, None], (3, n_local, part)),
            jnp.swapaxes(history_inner, 0, 1).reshape(3 * rows, n_local, part).astype(f32),
        ]
    ).reshape(8 + 3 * rows, chan)
    own_conv = lax.dynamic_slice_in_dim(conv_state_weight, hi, 1, 2)[:, :, 0]
    own_hist = lax.dynamic_slice_in_dim(history_state, hi, 1, 3)[:, :, :, 0].astype(f32)
    pack_bc = jnp.concatenate(
        [
            jnp.pad(own_conv, ((0, 4), (0, 0), (0, 0))),
            jnp.swapaxes(own_hist, 0, 1).reshape(3 * rows, 2, state_size),
        ]
    ).reshape(8 + 3 * rows, n_state)
    vmem = pl.BlockSpec(memory_space=pltpu.VMEM)
    hbm = pl.BlockSpec(memory_space=pl.ANY)
    shape = jax.ShapeDtypeStruct
    out, hidden, hist_x, hist_bc = pl.pallas_call(
        functools.partial(fused_kernel, n_mp, n_heads, n_local, per_head),
        out_shape=(
            shape((STEPS, rows, feat), f32),
            shape((rows, state_size, chan), f32),
            shape((3, rows, chan), f32),
            shape((n_heads, 3, rows, n_state), f32),
        ),
        in_specs=[vmem] * 5 + [hbm] * 5,
        out_specs=(vmem,) * 4,
        scratch_shapes=[
            pltpu.VMEM((n_heads, n_mp, 2, n_local, part, feat), bf16),
            pltpu.VMEM((n_heads, n_state, feat), bf16),
            pltpu.VMEM((n_heads, LANES, feat), bf16),
            pltpu.VMEM((n_mp, n_local, part, w_out.shape[2]), bf16),
            pltpu.VMEM((rows, feat), f32),
            pltpu.VMEM((n_heads, rows, feat), f32),
            pltpu.VMEM((n_mp, rows, 2 * chan + n_state + LANES), f32),
            pltpu.VMEM((n_mp, rows, 2 * chan + n_state + LANES), f32),
            pltpu.VMEM((rows, chan + LANES), f32),
            pltpu.VMEM((n_mp, rows, chan + LANES), f32),
            pltpu.VMEM((n_heads, rows, feat), f32),
            pltpu.VMEM((n_heads, rows, feat), f32),
            pltpu.VMEM((3, rows, n_state), f32),
            pltpu.VMEM((n_heads, 3, rows, n_state), f32),
            pltpu.VMEM((rows, chan), f32),
            pltpu.SemaphoreType.DMA((4 + n_mp, max(n_mp, n_heads))),
            pltpu.SemaphoreType.DMA((5, max(n_mp, n_heads))),
            pltpu.SemaphoreType.DMA((5, max(n_mp, n_heads))),
        ],
        compiler_params=pltpu.CompilerParams(
            collective_id=0, has_side_effects=True, vmem_limit_bytes=56 * 1024 * 1024
        ),
    )(
        stream.astype(f32),
        in_gain.reshape(n_heads, 1, feat),
        spread,
        pack,
        pack_bc,
        jnp.transpose(w_inner, (1, 2, 3, 0)),
        jnp.transpose(own_state),
        jnp.transpose(w_step),
        w_out,
        jnp.swapaxes(ssm_state.reshape(rows, chan, state_size), 1, 2),
    )
    hist_bc = hist_bc.reshape(n_groups, 3, rows, 2, state_size).transpose(2, 1, 3, 0, 4)
    return (
        out.astype(bf16),
        jnp.swapaxes(hidden, 1, 2).reshape(ssm_state.shape),
        jnp.swapaxes(hist_x, 0, 1).reshape(history_inner.shape).astype(bf16),
        hist_bc.astype(bf16),
    )


def choose_body(n_mp, n_heads):
    def run(*args):
        stream, w_inner, w_state, ssm_state = args[0], args[2], args[3], args[12]
        n_local, per_head = w_inner.shape[2], w_inner.shape[3]
        part = ssm_state.shape[2]
        aligned = (
            n_local == NH // NG
            and n_heads == w_state.shape[2]
            and n_local < LANES
            and n_local % 16 == 0
            and part % 16 == 0
            and stream.shape[0] % 8 == 0
            and LANES % part == 0
            and per_head == part * n_mp
            and (n_local * part) % LANES == 0
            and stream.shape[1] % LANES == 0
            and w_state.shape[3] % LANES == 0
        )
        if aligned:
            return fused_body(n_mp, n_heads, *args)
        return body(*args)

    return run


def solution(mesh):
    return jax.shard_map(
        choose_body(mesh.shape["mp"], mesh.shape["heads"]),
        mesh=mesh,
        in_specs=(
            P("groups", ("mp", "heads")),
            P("mp"),
            P("mp", None, "heads", None),
            P("mp", None, None, None),
            P("mp", "heads"),
            P("heads"),
            P("heads"),
            P("heads"),
            P(None, "heads", "mp"),
            P(),
            P("groups", None, "heads", "mp"),
            P("groups", None, None, None, None),
            P("groups", "heads", "mp", None),
            P("heads", "mp"),
            P("heads", None, "mp"),
        ),
        out_specs=(
            P(None, "groups", ("mp", "heads")),
            P("groups", "heads", "mp", None),
            P("groups", None, "heads", "mp"),
            P("groups", None, None, None, None),
        ),
        check_vma=False,
    )
```

```python
import functools

import jax
import jax.numpy as jnp
import numpy as np
from jax import lax
from jax.experimental import pallas as pl
from jax.experimental.pallas import tpu as pltpu
from jax.sharding import PartitionSpec as P

D = 8192
NH = 128
NG = 4
STEPS = 8


EPSILON = 1e-05


def causal_conv(history, incoming, kernel):
    window = jnp.concatenate([history, incoming[:, None]], axis=1)
    weighted = jnp.sum(window.astype(jnp.float32) * kernel[None], axis=1)
    return (jax.nn.silu(weighted), window[:, 1:])


def body(
    stream,
    in_gain,
    w_inner,
    w_state,
    w_step,
    step_bias,
    decay_scale,
    skip_gain,
    conv_inner,
    conv_state_weight,
    history_inner,
    history_state,
    ssm_state,
    norm_gain,
    w_out,
):
    row_count = stream.shape[0]
    local_width = w_inner.shape[0]
    local_heads = w_inner.shape[2]
    head_size = w_inner.shape[3]
    part_size = ssm_state.shape[2]
    group_count = w_state.shape[2]
    state_size = w_state.shape[3]
    flat_inner = w_inner.reshape(local_width, 2 * local_heads * head_size)
    flat_state = w_state.reshape(local_width, 2 * group_count * state_size)
    per_group = NH // NG
    head_ids = lax.axis_index("heads") * local_heads + jnp.arange(local_heads, dtype=jnp.int32)
    member = (head_ids // per_group)[:, None] == jnp.arange(group_count, dtype=jnp.int32)[None, :]
    current = stream
    hist_inner = history_inner
    hist_state = history_state
    hidden = ssm_state
    written = []
    for step_index in range(STEPS):
        values = lax.all_gather(current, "heads", axis=1, tiled=True).astype(jnp.float32)
        scaled = (values * in_gain[None, :]).astype(jnp.bfloat16)
        part_inner = jnp.dot(scaled, flat_inner, preferred_element_type=jnp.float32)
        part_state = jnp.dot(scaled, flat_state, preferred_element_type=jnp.float32)
        part_step = jnp.dot(scaled, w_step, preferred_element_type=jnp.float32)
        part_sq = jnp.sum(values * values, axis=1)
        summed_all, sum_state, sum_step, sum_sq = lax.psum(
            (part_inner, part_state, part_step, part_sq), "mp"
        )
        proj_inner = lax.dynamic_slice_in_dim(
            summed_all.reshape(row_count, 2, local_heads, head_size),
            lax.axis_index("mp") * part_size,
            part_size,
            3,
        )
        inv_rms = lax.rsqrt(sum_sq / D + EPSILON)[:, None]
        proj_inner = proj_inner * inv_rms[:, :, None, None]
        conv_x, hist_inner = causal_conv(
            hist_inner, proj_inner[:, 0].astype(jnp.bfloat16), conv_inner
        )
        incoming_bc = (
            (sum_state * inv_rms)
            .reshape(row_count, 2, group_count, state_size)
            .astype(jnp.bfloat16)
        )
        conv_bc, hist_state = causal_conv(hist_state, incoming_bc, conv_state_weight)
        head_b = jnp.sum(jnp.where(member[None, :, :, None], conv_bc[:, 0][:, None], 0.0), axis=2)
        head_c = jnp.sum(jnp.where(member[None, :, :, None], conv_bc[:, 1][:, None], 0.0), axis=2)
        step_dt = jax.nn.softplus(sum_step * inv_rms + step_bias[None, :])
        decay_rate = jnp.exp(-step_dt * decay_scale[None, :])
        hidden = (
            decay_rate[:, :, None, None] * hidden
            + (step_dt[:, :, None] * conv_x)[:, :, :, None] * head_b[:, :, None, :]
        )
        reading = (
            jnp.sum(hidden * head_c[:, :, None, :], axis=3) + skip_gain[None, :, None] * conv_x
        )
        gated_out = reading * jax.nn.silu(proj_inner[:, 1])
        head_sq = jnp.sum(gated_out * gated_out, axis=2)
        group_part = jnp.sum(jnp.where(member[None], head_sq[:, :, None], 0.0), axis=1)
        group_total = lax.psum(group_part, ("mp", "heads"))
        head_total = jnp.sum(jnp.where(member[None], group_total[:, None, :], 0.0), axis=2)
        mean_sq = head_total / (per_group * head_size)
        normed = (gated_out * lax.rsqrt(mean_sq + EPSILON)[:, :, None] * norm_gain[None]).astype(
            jnp.bfloat16
        )
        partial_out = jnp.einsum(
            "rhp,hpd->rd",
            lax.all_gather(normed, "mp", axis=2, tiled=True),
            w_out,
            preferred_element_type=jnp.float32,
        )
        update = lax.psum_scatter(partial_out, "heads", scatter_dimension=1, tiled=True)
        current = (current.astype(jnp.float32) + update).astype(jnp.bfloat16)
        written.append(current)
    return (jnp.stack(written), hidden, hist_inner, hist_state)


LANES = 128
MESH = pl.DeviceIdType.MESH


def silu(v):
    return v / (1.0 + jnp.exp(-v))


def fused_kernel(
    n_mp,
    n_heads,
    n_local,
    per_head,
    x_ref,
    gain_ref,
    spread_ref,
    pack_ref,
    pack_bc_ref,
    w_inner_hbm,
    w_state_hbm,
    w_step_hbm,
    w_out_hbm,
    state_hbm,
    out_ref,
    hidden,
    hist_x,
    hist_all,
    w_in,
    w_st,
    w_dt,
    w_o,
    current,
    gathered,
    parts,
    part_in,
    norm_out,
    norm_in,
    out_parts,
    out_in,
    hist_bc,
    hist_in,
    reading_s,
    load_sem,
    send_sem,
    recv_sem,
):
    mi = lax.axis_index("mp")
    hi = lax.axis_index("heads")
    rows, feat = x_ref.shape
    part = w_o.shape[2]
    chan = n_local * part
    n_state = w_st.shape[2]
    state_size = n_state // 2

    w_dt[...] = jnp.zeros_like(w_dt)
    loads_in = []
    for d in range(n_heads):
        owner = lax.rem(hi - d + n_heads, n_heads)
        span = pl.ds(pl.multiple_of(owner * feat, feat), feat)
        copies = [
            pltpu.make_async_copy(
                w_inner_hbm.at[:, :, m * part : (m + 1) * part, span],
                w_in.at[d, m],
                load_sem.at[4 + m, d],
            )
            for m in range(n_mp)
        ]
        copies.append(pltpu.make_async_copy(w_state_hbm.at[span], w_st.at[d], load_sem.at[0, d]))
        copies.append(
            pltpu.make_async_copy(
                w_step_hbm.at[:, span], w_dt.at[d, 0:n_local], load_sem.at[1, d]
            )
        )
        for c in copies:
            c.start()
        loads_in.append(copies)
    load_state = pltpu.make_async_copy(state_hbm, hidden, load_sem.at[2, 0])
    load_state.start()
    loads_out = []
    for d in range(n_mp):
        owner = lax.rem(mi - d + n_mp, n_mp)
        span = pl.ds(pl.multiple_of(owner * part, part), part)
        c = pltpu.make_async_copy(w_out_hbm.at[:, span], w_o.at[d], load_sem.at[3, d])
        c.start()
        loads_out.append(c)

    barrier = pltpu.get_barrier_semaphore()
    for d in range(1, n_heads):
        pl.semaphore_signal(
            barrier,
            inc=1,
            device_id={"heads": lax.rem(hi + d, n_heads)},
            device_id_type=MESH,
        )
    for d in range(1, n_mp):
        pl.semaphore_signal(
            barrier, inc=1, device_id={"mp": lax.rem(mi + d, n_mp)}, device_id_type=MESH
        )
    pl.semaphore_wait(barrier, n_heads + n_mp - 2)

    current[...] = x_ref[...]
    for k in range(3):
        hist_x[k] = pack_ref[8 + k * rows : 8 + (k + 1) * rows]
        hist_bc[k] = pack_bc_ref[8 + k * rows : 8 + (k + 1) * rows]

    def exchange(phase, axis, me, n, source, dest):
        copies = []
        for d in range(1, n):
            target = lax.rem(me + d, n)
            c = pltpu.make_async_remote_copy(
                src_ref=source(target),
                dst_ref=dest.at[d],
                send_sem=send_sem.at[phase, d],
                recv_sem=recv_sem.at[phase, d],
                device_id={axis: target},
                device_id_type=MESH,
            )
            c.start()
            copies.append(c)
        return copies

    def in_dot(x, w):
        return lax.dot_general(
            x, w, (((1,), (1,)), ((), ())), preferred_element_type=jnp.float32
        )

    def in_weight(d, m):
        return w_in[d, m].reshape(2 * chan, feat)

    def step(s, carry):
        cur = current[...]
        sent = exchange(0, "heads", hi, n_heads, lambda t: current, gathered)
        first = (cur * gain_ref[hi]).astype(jnp.bfloat16)
        sq = jnp.sum(cur * cur, axis=1, keepdims=True)

        @pl.when(s == 0)
        def _():
            for c in loads_in[0]:
                c.wait()

        for m in range(n_mp):
            parts[m, :, : 2 * chan] = in_dot(first, in_weight(0, m))
        aux = jnp.dot(first, w_st[0], preferred_element_type=jnp.float32)
        tail = in_dot(first, w_dt[0])
        later = []
        for d in range(1, n_heads):
            sent[d - 1].wait()
            v = gathered[d]
            owner = lax.rem(hi - d + n_heads, n_heads)
            later.append((v * gain_ref[owner]).astype(jnp.bfloat16))
            sq = sq + jnp.sum(v * v, axis=1, keepdims=True)

        @pl.when(s == 0)
        def _():
            for copies in loads_in[1:]:
                for c in copies:
                    c.wait()

        for m in range(n_mp):
            total = parts[m, :, : 2 * chan]
            for d in range(1, n_heads):
                total = total + in_dot(later[d - 1], in_weight(d, m))
            parts[m, :, : 2 * chan] = total
        for d in range(1, n_heads):
            aux = aux + jnp.dot(later[d - 1], w_st[d], preferred_element_type=jnp.float32)
            tail = tail + in_dot(later[d - 1], w_dt[d])
        lane = lax.broadcasted_iota(jnp.int32, (rows, LANES), 1)
        tail = jnp.where(lane == n_local, sq, tail)
        for m in range(n_mp):
            parts[m, :, 2 * chan : 2 * chan + n_state] = aux
            parts[m, :, 2 * chan + n_state :] = tail

        sent = exchange(1, "mp", mi, n_mp, lambda t: parts.at[t], part_in)
        total = parts[mi]
        for d in range(1, n_mp):
            sent[d - 1].wait()
            total = total + part_in[d]
        tail = total[:, 2 * chan + n_state :]
        inv = lax.rsqrt(tail[:, n_local : n_local + 1] / D + EPSILON)
        new_x = (total[:, :chan] * inv).astype(jnp.bfloat16).astype(jnp.float32)
        gate = total[:, chan : 2 * chan] * inv
        new_bc = (
            (total[:, 2 * chan : 2 * chan + n_state] * inv)
            .astype(jnp.bfloat16)
            .astype(jnp.float32)
        )

        def conv(hist, new, kernel):
            old = [hist[0], hist[1], hist[2]]
            hist[0] = old[1]
            hist[1] = old[2]
            hist[2] = new
            v = old[0] * kernel[0:1] + old[1] * kernel[1:2] + old[2] * kernel[2:3] + new * kernel[3:4]
            return silu(v)

        conv_x = conv(hist_x, new_x, pack_ref)
        conv_bc = conv(hist_bc, new_bc, pack_bc_ref)
        spread = jnp.dot(
            tail,
            spread_ref[...],
            preferred_element_type=jnp.float32,
            precision=lax.Precision.HIGHEST,
        )
        raw = spread * inv + pack_ref[5:6]
        dt = jnp.maximum(raw, 0.0) + jnp.log1p(jnp.exp(-jnp.abs(raw)))
        decay = jnp.exp(-dt * pack_ref[6:7])
        driven = dt * conv_x
        b_cols = jnp.transpose(conv_bc[:, :state_size])
        c_cols = jnp.transpose(conv_bc[:, state_size:])
        part_n = min(state_size, 64)

        @pl.when(s == 0)
        def _():
            load_state.wait()

        for r in range(rows):
            sums = [jnp.zeros((part_n, LANES), jnp.float32) for _ in range(chan // LANES)]
            for n0 in range(0, state_size, part_n):
                b_wide = jnp.broadcast_to(b_cols[n0 : n0 + part_n, r : r + 1], (part_n, LANES))
                c_wide = jnp.broadcast_to(c_cols[n0 : n0 + part_n, r : r + 1], (part_n, LANES))
                for c in range(chan // LANES):
                    cols = slice(c * LANES, (c + 1) * LANES)
                    h = (
                        decay[r : r + 1, cols] * hidden[r, n0 : n0 + part_n, cols]
                        + driven[r : r + 1, cols] * b_wide
                    )
                    hidden[r, n0 : n0 + part_n, cols] = h
                    sums[c] = sums[c] + h * c_wide
            for c in range(chan // LANES):
                reading_s[r : r + 1, c * LANES : (c + 1) * LANES] = jnp.sum(
                    sums[c], axis=0, keepdims=True
                )
        reading = reading_s[...] + pack_ref[7:8] * conv_x
        gated = reading * silu(gate)
        group_sq = jnp.sum(gated * gated, axis=1, keepdims=True)
        mine = (gated * pack_ref[4:5]).astype(jnp.bfloat16)
        norm_out[:, :chan] = mine.astype(jnp.float32)
        norm_out[:, chan:] = jnp.broadcast_to(group_sq, (rows, LANES))

        sent = exchange(2, "mp", mi, n_mp, lambda t: norm_out, norm_in)

        def out_weight(d, b):
            w = w_o[d, :, :, b * feat : (b + 1) * feat]
            return w.reshape(w.shape[0] * w.shape[1], feat)

        @pl.when(s == 0)
        def _():
            for c in loads_out:
                c.wait()

        for b in range(n_heads):
            out_parts[b] = jnp.dot(mine, out_weight(0, b), preferred_element_type=jnp.float32)
        later = []
        for d in range(1, n_mp):
            sent[d - 1].wait()
            later.append(norm_in[d, :, :chan].astype(jnp.bfloat16))
            group_sq = group_sq + norm_in[d, :, chan : chan + 1]
        scale = lax.rsqrt(group_sq / (n_local * per_head) + EPSILON)
        for b in range(n_heads):
            total = out_parts[b]
            for d in range(1, n_mp):
                total = total + jnp.dot(
                    later[d - 1], out_weight(d, b), preferred_element_type=jnp.float32
                )
            out_parts[b] = total * scale

        sent = exchange(3, "heads", hi, n_heads, lambda t: out_parts.at[t], out_in)
        update = out_parts[hi]
        for d in range(1, n_heads):
            sent[d - 1].wait()
            update = update + out_in[d]
        new = (cur + update).astype(jnp.bfloat16).astype(jnp.float32)
        current[...] = new
        out_ref[s] = new
        return carry

    lax.fori_loop(0, STEPS, step, 0)

    sent = exchange(4, "heads", hi, n_heads, lambda t: hist_bc, hist_in)
    hist_all[hi] = hist_bc[...]
    for d in range(1, n_heads):
        sent[d - 1].wait()
        hist_all[lax.rem(hi - d + n_heads, n_heads)] = hist_in[d]


def fused_body(
    n_mp,
    n_heads,
    stream,
    in_gain,
    w_inner,
    w_state,
    w_step,
    step_bias,
    decay_scale,
    skip_gain,
    conv_inner,
    conv_state_weight,
    history_inner,
    history_state,
    ssm_state,
    norm_gain,
    w_out,
):
    f32, bf16 = jnp.float32, jnp.bfloat16
    rows, feat = stream.shape
    width, _, n_local, per_head = w_inner.shape
    part = ssm_state.shape[2]
    state_size = w_state.shape[3]
    n_groups = w_state.shape[2]
    chan = n_local * part
    n_state = 2 * state_size
    hi = lax.axis_index("heads")
    spread = (np.arange(LANES)[:, None] == (np.arange(chan) // part)[None, :]).astype(np.float32)
    chosen = (jnp.arange(n_groups) == hi)[None, :, None]
    own_state = jnp.concatenate(
        [
            jnp.sum(jnp.where(chosen, w_state[:, k].astype(f32), 0.0), axis=1).astype(bf16)
            for k in range(2)
        ],
        axis=1,
    )
    heads_wide = jnp.stack([step_bias, decay_scale, skip_gain])
    pack = jnp.concatenate(
        [
            conv_inner,
            norm_gain[None],
            jnp.broadcast_to(heads_wide[:, :, None], (3, n_local, part)),
            jnp.swapaxes(history_inner, 0, 1).reshape(3 * rows, n_local, part).astype(f32),
        ]
    ).reshape(8 + 3 * rows, chan)
    own_conv = lax.dynamic_slice_in_dim(conv_state_weight, hi, 1, 2)[:, :, 0]
    own_hist = lax.dynamic_slice_in_dim(history_state, hi, 1, 3)[:, :, :, 0].astype(f32)
    pack_bc = jnp.concatenate(
        [
            jnp.pad(own_conv, ((0, 4), (0, 0), (0, 0))),
            jnp.swapaxes(own_hist, 0, 1).reshape(3 * rows, 2, state_size),
        ]
    ).reshape(8 + 3 * rows, n_state)
    vmem = pl.BlockSpec(memory_space=pltpu.VMEM)
    hbm = pl.BlockSpec(memory_space=pl.ANY)
    shape = jax.ShapeDtypeStruct
    out, hidden, hist_x, hist_bc = pl.pallas_call(
        functools.partial(fused_kernel, n_mp, n_heads, n_local, per_head),
        out_shape=(
            shape((STEPS, rows, feat), f32),
            shape((rows, state_size, chan), f32),
            shape((3, rows, chan), f32),
            shape((n_heads, 3, rows, n_state), f32),
        ),
        in_specs=[vmem] * 5 + [hbm] * 5,
        out_specs=(vmem,) * 4,
        scratch_shapes=[
            pltpu.VMEM((n_heads, n_mp, 2, n_local, part, feat), bf16),
            pltpu.VMEM((n_heads, feat, n_state), bf16),
            pltpu.VMEM((n_heads, LANES, feat), bf16),
            pltpu.VMEM((n_mp, n_local, part, w_out.shape[2]), bf16),
            pltpu.VMEM((rows, feat), f32),
            pltpu.VMEM((n_heads, rows, feat), f32),
            pltpu.VMEM((n_mp, rows, 2 * chan + n_state + LANES), f32),
            pltpu.VMEM((n_mp, rows, 2 * chan + n_state + LANES), f32),
            pltpu.VMEM((rows, chan + LANES), f32),
            pltpu.VMEM((n_mp, rows, chan + LANES), f32),
            pltpu.VMEM((n_heads, rows, feat), f32),
            pltpu.VMEM((n_heads, rows, feat), f32),
            pltpu.VMEM((3, rows, n_state), f32),
            pltpu.VMEM((n_heads, 3, rows, n_state), f32),
            pltpu.VMEM((rows, chan), f32),
            pltpu.SemaphoreType.DMA((4 + n_mp, max(n_mp, n_heads))),
            pltpu.SemaphoreType.DMA((5, max(n_mp, n_heads))),
            pltpu.SemaphoreType.DMA((5, max(n_mp, n_heads))),
        ],
        compiler_params=pltpu.CompilerParams(
            collective_id=0, has_side_effects=True, vmem_limit_bytes=56 * 1024 * 1024
        ),
    )(
        stream.astype(f32),
        in_gain.reshape(n_heads, 1, feat),
        spread,
        pack,
        pack_bc,
        jnp.transpose(w_inner, (1, 2, 3, 0)),
        own_state,
        jnp.transpose(w_step),
        w_out,
        jnp.swapaxes(ssm_state.reshape(rows, chan, state_size), 1, 2),
    )
    hist_bc = hist_bc.reshape(n_groups, 3, rows, 2, state_size).transpose(2, 1, 3, 0, 4)
    return (
        out.astype(bf16),
        jnp.swapaxes(hidden, 1, 2).reshape(ssm_state.shape),
        jnp.swapaxes(hist_x, 0, 1).reshape(history_inner.shape).astype(bf16),
        hist_bc.astype(bf16),
    )


def choose_body(n_mp, n_heads):
    def run(*args):
        stream, w_inner, w_state, ssm_state = args[0], args[2], args[3], args[12]
        n_local, per_head = w_inner.shape[2], w_inner.shape[3]
        part = ssm_state.shape[2]
        aligned = (
            n_local == NH // NG
            and n_heads == w_state.shape[2]
            and n_local < LANES
            and n_local % 16 == 0
            and part % 16 == 0
            and stream.shape[0] % 8 == 0
            and LANES % part == 0
            and per_head == part * n_mp
            and (n_local * part) % LANES == 0
            and stream.shape[1] % LANES == 0
            and w_state.shape[3] % LANES == 0
        )
        if aligned:
            return fused_body(n_mp, n_heads, *args)
        return body(*args)

    return run


def solution(mesh):
    return jax.shard_map(
        choose_body(mesh.shape["mp"], mesh.shape["heads"]),
        mesh=mesh,
        in_specs=(
            P("groups", ("mp", "heads")),
            P("mp"),
            P("mp", None, "heads", None),
            P("mp", None, None, None),
            P("mp", "heads"),
            P("heads"),
            P("heads"),
            P("heads"),
            P(None, "heads", "mp"),
            P(),
            P("groups", None, "heads", "mp"),
            P("groups", None, None, None, None),
            P("groups", "heads", "mp", None),
            P("heads", "mp"),
            P("heads", None, "mp"),
        ),
        out_specs=(
            P(None, "groups", ("mp", "heads")),
            P("groups", "heads", "mp", None),
            P("groups", None, "heads", "mp"),
            P("groups", None, None, None, None),
        ),
        check_vma=False,
    )
```
